256 devices in a mesh: dp: 4 (over x), fsdp: 64 (over z, y, core).
Axes of the slice: x: 4, y: 4, z: 8, core: 2. Of those that a mesh axis runs over, the one named last changes fastest.
Arguments:
- grads: bfloat16 [4, 256, 512, 512], P('dp', None, 'fsdp'), may hold values from -32 to 32
- order: int32 [256], replicated, may hold values from 0 to 255, each once
- prev_roots: float32 [256, 2, 512, 512], P(('dp', 'fsdp')), may hold values from -1 to 3, as said below
Outputs:
- precond: bfloat16 [256, 512, 512], P(None, 'fsdp')
- new_roots: float32 [256, 2, 512, 512], P(('dp', 'fsdp'))
The draws below stay inside these ranges and needn't reach their ends.
Inputs may be any that keep to these rules, and one draw needn't show every extreme that they name: `prev_roots`: each block is a symmetric matrix.
All inputs are finite; a program needn't handle non-finite values.
Results may differ from the reference program's by a relative error of at most 0.001.
Values may be sent and summed in bfloat16 or wider, within the bound.
No kernel may reach another device: no remote copies, remote signals or barrier semaphores. Data moves between devices by JAX's collectives and lax.ppermute only.
A program may use at most 128 MiB of HBM per device.

```python
import math
import jax
import jax.numpy as jnp
from jax import lax

ORDER = 512
ITERS = 3
MICRO = 4
NBLK = 256


def draw_grads(key, part):
    key = jax.random.fold_in(key, 11)
    key_one = jax.random.fold_in(key, 0)
    full_shape = (MICRO, NBLK, ORDER, ORDER)
    values = jax.random.truncated_normal(key_one, -4.5, 4.5, full_shape, jnp.float32)
    return values.astype(jnp.bfloat16)


def draw_prev_roots(key, part):
    key = jax.random.fold_in(key, 23)
    key_one, key_two = jax.random.split(key, 2)
    full_shape = (NBLK, 2, ORDER, ORDER)
    spread = 0.15 * ORDER ** (-0.5)
    strength = 0.7
    perturbation = jax.random.truncated_normal(key_one, -6.0, 6.0, full_shape, jnp.float32) * spread
    center = (strength * math.sqrt(ORDER * (1.0 + 1.0 / MICRO))) ** 0.25
    symmetric = (perturbation + jnp.swapaxes(perturbation, -1, -2)) * math.sqrt(0.5)
    diagonal = jax.random.uniform(key_two, (NBLK, 2, ORDER, 1), jnp.float32, 0.85, 1.0)
    on_diagonal = jnp.eye(ORDER, dtype=bool)
    return (center * jnp.where(on_diagonal, diagonal, symmetric)).astype(jnp.float32)


def setup_inputs(seed: int = 0) -> dict:
    seeds = jax.random.split(jax.random.key(seed), 4)
    grads = draw_grads(jax.random.fold_in(seeds[3], 71), 0)
    order = jax.random.permutation(seeds[1], NBLK).astype(jnp.int32)
    prev_roots = draw_prev_roots(jax.random.fold_in(seeds[3], 71), 0)
    return dict(grads=grads, order=order, prev_roots=prev_roots)


def product(left_side, right_side):
    return jnp.einsum('...ij,...jk->...ik', left_side, right_side, precision=lax.Precision.HIGHEST, preferred_element_type=jnp.float32)

def inverse_root(previous, statistic):
    width = statistic.shape[-1]
    frobenius = jnp.sqrt(lax.optimization_barrier(jnp.mean(statistic * statistic, axis=(-2, -1), keepdims=True)) + 1e-06) * width
    scaled = statistic / frobenius
    identity = jnp.eye(width, dtype=jnp.float32)
    square = product(previous, previous)
    fourth = product(square, square)
    moment = product(fourth, scaled)
    root = previous
    for step in range(ITERS):
        factor = (5.0 * identity - moment) * 0.25
        root = product(root, factor)
        if step + 1 < ITERS:
            factor_sq = product(factor, factor)
            moment = product(product(factor_sq, factor_sq), moment)
    return root

def reference(grads, order, prev_roots):

    def refresh(position):
        block = order[position]
        pieces = lax.dynamic_index_in_dim(grads, block, 1, keepdims=False)
        left_stat = jnp.zeros((ORDER, ORDER), jnp.float32)
        right_stat = jnp.zeros((ORDER, ORDER), jnp.float32)
        total = jnp.zeros((ORDER, ORDER), jnp.float32)
        for micro in range(MICRO):
            piece = pieces[micro]
            left_stat = left_stat + jnp.dot(piece, piece.T, preferred_element_type=jnp.float32)
            right_stat = right_stat + jnp.dot(piece.T, piece, preferred_element_type=jnp.float32)
            total = total + piece.astype(jnp.float32)
        mean_grad = total / MICRO
        roots = lax.dynamic_index_in_dim(prev_roots, position, 0, keepdims=False)
        root_left = inverse_root(roots[0], left_stat)
        root_right = inverse_root(roots[1], right_stat)
        result = product(product(root_left, mean_grad), root_right).astype(jnp.bfloat16)
        return (result, jnp.stack([root_left, root_right]))
    by_position, new_roots = lax.map(refresh, jnp.arange(NBLK, dtype=jnp.int32))
    precond = jnp.zeros_like(by_position).at[order].set(by_position)
    return (precond, new_roots)
```

```python
import jax
import jax.numpy as jnp
from jax import lax
from jax.sharding import PartitionSpec as P

ITERS = 3


def product(left_side, right_side):
    return jnp.einsum(
        "...ij,...jk->...ik",
        left_side,
        right_side,
        precision=lax.Precision.HIGH,
        preferred_element_type=jnp.float32,
    )


def inverse_root(previous, statistic):
    width = statistic.shape[-1]
    frobenius = (
        jnp.sqrt(jnp.mean(statistic * statistic, axis=(-2, -1), keepdims=True) + 1e-06) * width
    )
    scaled = statistic / frobenius
    identity = jnp.eye(width, dtype=jnp.float32)
    square = product(previous, previous)
    fourth = product(square, square)
    moment = product(fourth, scaled)
    root = previous
    for step in range(ITERS):
        factor = (5.0 * identity - moment) * 0.25
        root = product(root, factor)
        if step + 1 < ITERS:
            factor_sq = product(factor, factor)
            moment = product(product(factor_sq, factor_sq), moment)
    return root


def body(grads, order, prev_roots):
    n_data = lax.axis_size("dp")
    local = grads[0]
    width = local.shape[2]
    outgoing = local.at[order].get(mode="promise_in_bounds", unique_indices=True)
    arrived = lax.all_to_all(outgoing, ("dp", "fsdp"), split_axis=0, concat_axis=0, tiled=True)
    arrived = arrived.reshape(n_data, width, width)
    left_stat = jnp.einsum("dij,dkj->ik", arrived, arrived, preferred_element_type=jnp.float32)
    right_stat = jnp.einsum("dji,djk->ik", arrived, arrived, preferred_element_type=jnp.float32)
    mean_grad = jnp.sum(arrived, axis=0, dtype=jnp.float32) / n_data
    root_left = inverse_root(prev_roots[0, 0], left_stat)
    root_right = inverse_root(prev_roots[0, 1], right_stat)
    new_roots = jnp.stack([root_left, root_right], axis=0)[None]
    refreshed = product(product(root_left, mean_grad), root_right).astype(jnp.bfloat16)
    rows = local.shape[1]
    pieces = refreshed.reshape(width // rows, rows, width)
    mine = lax.all_to_all(pieces, "fsdp", split_axis=0, concat_axis=0, tiled=True)
    back = lax.all_gather(mine, "dp", axis=0, tiled=True)
    positions = jnp.arange(order.shape[0], dtype=jnp.int32)
    inverse = jnp.zeros_like(order).at[order].set(
        positions, mode="promise_in_bounds", unique_indices=True
    )
    result = back.at[inverse].get(mode="promise_in_bounds", unique_indices=True)
    return (result, new_roots)


def solution(mesh):
    return jax.shard_map(
        body,
        mesh=mesh,
        in_specs=(P("dp", None, "fsdp", None), P(), P(("dp", "fsdp"), None, None, None)),
        out_specs=(P(None, "fsdp", None), P(("dp", "fsdp"), None, None, None)),
        check_vma=False,
    )
```

```python
import functools

import jax
import jax.numpy as jnp
from jax import lax
from jax.experimental import pallas as pl
from jax.experimental.pallas import tpu as pltpu
from jax.sharding import PartitionSpec as P

ITERS = 3
MB = 1 << 20
BF16 = jnp.bfloat16
F32 = jnp.float32
ANY = pl.BlockSpec(memory_space=pl.ANY)
VMEM = pl.BlockSpec(memory_space=pltpu.VMEM)
SMEM = pl.BlockSpec(memory_space=pltpu.SMEM)


def split(value):
    high = value.astype(BF16)
    return high, (value - high.astype(F32)).astype(BF16)


def product3(lhs, rhs, rows):
    high = lhs[0, rows, :]
    left = jnp.concatenate([high, lhs[1, rows, :], high], axis=1)
    over = rhs[0]
    right = jnp.concatenate([over, over, rhs[1]], axis=0)
    return jnp.dot(left, right, preferred_element_type=F32)


def keep(target, rows, value):
    high, low = split(value)
    target[0, rows, :] = high
    target[1, rows, :] = low


def halves(width):
    size = width // 2
    return [pl.ds(0, size), pl.ds(size, size)]


def fourth_kernel(prev, x_out, q_out, square):
    width = prev.shape[-1]
    for side in range(2):
        keep(x_out.at[side], slice(None), prev[side])
    for source, target in ((x_out, square), (square, q_out)):
        for rows in halves(width):
            for side in range(2):
                keep(target.at[side], rows, product3(source.at[side], source.at[side], rows))


def fourth_powers(prev):
    width = prev.shape[-1]
    pair = jax.ShapeDtypeStruct((2, 2, width, width), BF16)
    return pl.pallas_call(
        fourth_kernel,
        out_shape=(pair, pair),
        in_specs=[VMEM],
        out_specs=(VMEM, VMEM),
        scratch_shapes=[pltpu.VMEM((2, 2, width, width), BF16)],
        compiler_params=pltpu.CompilerParams(vmem_limit_bytes=20 * MB),
        cost_estimate=pl.CostEstimate(
            flops=2 * 2 * 3 * 2 * width**3, bytes_accessed=6 * MB, transcendentals=0
        ),
        name="fourth_powers",
    )(prev)


def refresh_kernel(
    arrived, x, q, roots, out, stat, moment, factor, power, root, mean, mixed
):
    n_micro, width = arrived.shape[0], arrived.shape[-1]
    parts = halves(width)
    size = width // 2
    scales = []
    whole = [arrived[d] for d in range(n_micro)]
    for side in range(2):
        total = jnp.zeros((1, 1), F32)
        if side == 0:
            rhs = jnp.concatenate(whole, axis=1)
            contract = (((1,), (1,)), ((), ()))
        else:
            rhs = jnp.concatenate(whole, axis=0)
            contract = (((0,), (0,)), ((), ()))
        for index, rows in enumerate(parts):
            lo = index * size
            hi = lo + size
            lhs = rhs[lo:hi, :] if side == 0 else rhs[:, lo:hi]
            value = lax.dot_general(lhs, rhs, contract, preferred_element_type=F32)
            total = total + jnp.sum(value * value, axis=(0, 1), keepdims=True)
            keep(stat.at[side], rows, value)
        scales.append(1.0 / (jnp.sqrt(total / (width * width) + 1e-06) * width))
    for index, rows in enumerate(parts):
        lo = index * size
        value = whole[0][lo : lo + size].astype(F32)
        for d in range(1, n_micro):
            value = value + whole[d][lo : lo + size].astype(F32)
        keep(mean, rows, value / n_micro)

    row_ids = lax.broadcasted_iota(jnp.int32, (size, width), 0)
    col_ids = lax.broadcasted_iota(jnp.int32, (size, width), 1)

    def keep_factor(side, index, rows, value):
        diagonal = jnp.where(row_ids + index * size == col_ids, 1.25, 0.0)
        keep(factor.at[side], rows, diagonal - 0.25 * value)

    for index, rows in enumerate(parts):
        for side in range(2):
            value = product3(q.at[side], stat.at[side], rows) * scales[side]
            keep(moment.at[0, side], rows, value)
            keep_factor(side, index, rows, value)
    held = x
    for step in range(ITERS - 1):
        for rows in parts:
            for side in range(2):
                keep(
                    power.at[0, side], rows, product3(factor.at[side], factor.at[side], rows)
                )
        for rows in parts:
            for side in range(2):
                keep(
                    root.at[step % 2, side], rows, product3(held.at[side], factor.at[side], rows)
                )
        held = root.at[step % 2]
        for rows in parts:
            for side in range(2):
                keep(
                    power.at[1, side],
                    rows,
                    product3(power.at[0, side], power.at[0, side], rows),
                )
        for index, rows in enumerate(parts):
            for side in range(2):
                value = product3(power.at[1, side], moment.at[step % 2, side], rows)
                if step + 2 < ITERS:
                    keep(moment.at[(step + 1) % 2, side], rows, value)
                keep_factor(side, index, rows, value)
    final = root.at[(ITERS - 1) % 2]
    for side in range(2):
        for rows in parts:
            value = product3(held.at[side], factor.at[side], rows)
            roots[side, rows, :] = value
            keep(final.at[side], rows, value)
    for rows in parts:
        keep(mixed, rows, product3(final.at[0], mean, rows))
    for rows in parts:
        out[rows, :] = product3(mixed, final.at[1], rows).astype(BF16)


def refresh(arrived, x, q):
    width = arrived.shape[-1]
    matrix = (2, 2, width, width)
    return pl.pallas_call(
        refresh_kernel,
        out_shape=(
            jax.ShapeDtypeStruct((2, width, width), F32),
            jax.ShapeDtypeStruct((width, width), BF16),
        ),
        in_specs=[VMEM, VMEM, VMEM],
        out_specs=(VMEM, VMEM),
        scratch_shapes=[
            pltpu.VMEM(matrix, BF16),
            pltpu.VMEM((2,) + matrix, BF16),
            pltpu.VMEM(matrix, BF16),
            pltpu.VMEM((2,) + matrix, BF16),
            pltpu.VMEM((2,) + matrix, BF16),
            pltpu.VMEM((2, width, width), BF16),
            pltpu.VMEM((2, width, width), BF16),
        ],
        compiler_params=pltpu.CompilerParams(vmem_limit_bytes=36 * MB),
        cost_estimate=pl.CostEstimate(
            flops=(22 * 3 + 8) * 2 * width**3, bytes_accessed=9 * MB, transcendentals=0
        ),
        name="refresh_roots",
    )(arrived, x, q)


def place_kernel(owners, offset, order, source, *rest):
    out, sem = rest[-2:]
    blocks = source.shape[0]
    base = lax.rem(lax.axis_index("dp") + offset[0], lax.axis_size("dp")) * owners + offset[1]

    def step(i, _):
        pltpu.make_async_copy(source.at[i], out.at[order[base + i]], sem).start()
        return 0

    lax.fori_loop(0, blocks, step, 0, unroll=8)
    pltpu.make_async_copy(source, out.at[pl.ds(0, blocks)], sem).wait()


def place(owners, offset, order, source, base):
    rows, width = source.shape[1:]
    args, specs, aliases = [order, source], [SMEM, VMEM], {}
    if base is not None:
        args.append(base)
        specs.append(ANY)
        aliases = {2: 0}
    return pl.pallas_call(
        functools.partial(place_kernel, owners, offset),
        out_shape=jax.ShapeDtypeStruct((order.shape[0], rows, width), source.dtype),
        in_specs=specs,
        out_specs=ANY,
        scratch_shapes=[pltpu.SemaphoreType.DMA(())],
        input_output_aliases=aliases,
        compiler_params=pltpu.CompilerParams(vmem_limit_bytes=8 * MB),
        cost_estimate=pl.CostEstimate(
            flops=0, bytes_accessed=4 * source.size, transcendentals=0
        ),
        name="place_blocks",
    )(*args)


def body(grads, order, prev_roots):
    n_data = lax.axis_size("dp")
    local = grads[0]
    rows, width = local.shape[1:]
    outgoing = local.at[order].get(
        mode="promise_in_bounds", unique_indices=True, wrap_negative_indices=False
    )
    arrived = lax.all_to_all(outgoing, ("dp", "fsdp"), split_axis=0, concat_axis=0, tiled=True)
    x, q = fourth_powers(prev_roots[0])
    roots, refreshed = refresh(arrived.reshape(n_data, width, width), x, q)
    pieces = refreshed.reshape(width // rows, rows, width)
    mine = lax.all_to_all(pieces, "fsdp", split_axis=0, concat_axis=0, tiled=True)
    owners = mine.shape[0]
    half = owners // 2

    def shift(value, by):
        return lax.ppermute(value, "dp", [(i, (i + by) % n_data) for i in range(n_data)])

    low, high = mine[:half], mine[half:]
    low_up, high_down = shift(low, 1), shift(high, -1)
    high_up, low_down = shift(high, 1), shift(low, -1)
    low_far, high_far = shift(low_up, 1), shift(high_down, -1)
    result = None
    for offset, piece in (
        ((0, 0), mine),
        ((n_data - 1, 0), low_up),
        ((1, half), high_down),
        ((n_data - 1, half), high_up),
        ((1, 0), low_down),
        ((n_data - 2, 0), low_far),
        ((2, half), high_far),
    ):
        result = place(owners, offset, order, piece, result)
    return (result, roots[None])


def solution(mesh):
    return jax.shard_map(
        body,
        mesh=mesh,
        in_specs=(P("dp", None, "fsdp", None), P(), P(("dp", "fsdp"), None, None, None)),
        out_specs=(P(None, "fsdp", None), P(("dp", "fsdp"), None, None, None)),
        check_vma=False,
    )
```

```python
import functools

import jax
import jax.numpy as jnp
from jax import lax
from jax.experimental import pallas as pl
from jax.experimental.pallas import tpu as pltpu
from jax.sharding import Mesh, PartitionSpec as P

ITERS = 3
MB = 1 << 20
REFRESH_MB = 32
BF16 = jnp.bfloat16
F32 = jnp.float32
ANY = pl.BlockSpec(memory_space=pl.ANY)
VMEM = pl.BlockSpec(memory_space=pltpu.VMEM)
SMEM = pl.BlockSpec(memory_space=pltpu.SMEM)


def split(value):
    high = value.astype(BF16)
    return high, (value - high.astype(F32)).astype(BF16)


def product3(lhs, rhs, rows):
    high = lhs[0, rows, :]
    left = jnp.concatenate([high, lhs[1, rows, :], high], axis=1)
    over = rhs[0]
    right = jnp.concatenate([over, over, rhs[1]], axis=0)
    return jnp.dot(left, right, preferred_element_type=F32)


def keep(target, rows, value):
    high, low = split(value)
    target[0, rows, :] = high
    target[1, rows, :] = low


def halves(width):
    size = width // 2
    return [pl.ds(0, size), pl.ds(size, size)]


def fourth_kernel(prev, x_out, q_out, square):
    width = prev.shape[-1]
    for side in range(2):
        keep(x_out.at[side], slice(None), prev[side])
    for source, target in ((x_out, square), (square, q_out)):
        for rows in halves(width):
            for side in range(2):
                keep(target.at[side], rows, product3(source.at[side], source.at[side], rows))


def fourth_powers(prev):
    width = prev.shape[-1]
    pair = jax.ShapeDtypeStruct((2, 2, width, width), BF16)
    return pl.pallas_call(
        fourth_kernel,
        out_shape=(pair, pair),
        in_specs=[VMEM],
        out_specs=(VMEM, VMEM),
        scratch_shapes=[pltpu.VMEM((2, 2, width, width), BF16)],
        compiler_params=pltpu.CompilerParams(vmem_limit_bytes=20 * MB),
        cost_estimate=pl.CostEstimate(
            flops=2 * 2 * 3 * 2 * width**3, bytes_accessed=6 * MB, transcendentals=0
        ),
        name="fourth_powers",
    )(prev)


def refresh_kernel(n_z, *refs):
    near, (far, x, q, roots, out) = refs[:n_z], refs[n_z : n_z + 5]
    grads, stat, moment, factor, power, root, mean, mixed = refs[n_z + 5 :]
    n_micro, width = grads.shape[0], grads.shape[-1]
    parts = halves(width)
    size = width // 2
    plane = near[0].shape[0] // n_micro
    z = lax.axis_index("z")
    for shift in range(n_z):
        source = lax.rem(z + (n_z - shift), n_z)
        rows = pl.ds(pl.multiple_of(source * (width // n_z), width // n_z), width // n_z)
        for d in range(n_micro):
            senders = pl.ds(d * plane, plane)
            for column, piece in enumerate((near[shift][senders], far[senders, shift])):
                joined = piece.astype(F32).reshape(width // n_z, size).astype(BF16)
                grads[d, rows, pl.ds(column * size, size)] = joined
    scales = []
    whole = [grads[d] for d in range(n_micro)]
    for side in range(2):
        total = jnp.zeros((1, 1), F32)
        if side == 0:
            rhs = jnp.concatenate(whole, axis=1)
            contract = (((1,), (1,)), ((), ()))
        else:
            rhs = jnp.concatenate(whole, axis=0)
            contract = (((0,), (0,)), ((), ()))
        for index, rows in enumerate(parts):
            lo = index * size
            hi = lo + size
            lhs = rhs[lo:hi, :] if side == 0 else rhs[:, lo:hi]
            value = lax.dot_general(lhs, rhs, contract, preferred_element_type=F32)
            total = total + jnp.sum(value * value, axis=(0, 1), keepdims=True)
            keep(stat.at[side], rows, value)
        scales.append(1.0 / (jnp.sqrt(total / (width * width) + 1e-06) * width))
    for index, rows in enumerate(parts):
        lo = index * size
        value = whole[0][lo : lo + size].astype(F32)
        for d in range(1, n_micro):
            value = value + whole[d][lo : lo + size].astype(F32)
        keep(mean, rows, value / n_micro)

    row_ids = lax.broadcasted_iota(jnp.int32, (size, width), 0)
    col_ids = lax.broadcasted_iota(jnp.int32, (size, width), 1)

    def keep_factor(side, index, rows, value):
        diagonal = jnp.where(row_ids + index * size == col_ids, 1.25, 0.0)
        keep(factor.at[side], rows, diagonal - 0.25 * value)

    for index, rows in enumerate(parts):
        for side in range(2):
            value = product3(q.at[side], stat.at[side], rows) * scales[side]
            keep(moment.at[0, side], rows, value)
            keep_factor(side, index, rows, value)
    held = x
    for step in range(ITERS - 1):
        for rows in parts:
            for side in range(2):
                keep(
                    power.at[0, side], rows, product3(factor.at[side], factor.at[side], rows)
                )
        for rows in parts:
            for side in range(2):
                keep(
                    root.at[step % 2, side], rows, product3(held.at[side], factor.at[side], rows)
                )
        held = root.at[step % 2]
        for rows in parts:
            for side in range(2):
                keep(
                    power.at[1, side],
                    rows,
                    product3(power.at[0, side], power.at[0, side], rows),
                )
        for index, rows in enumerate(parts):
            for side in range(2):
                value = product3(power.at[1, side], moment.at[step % 2, side], rows)
                if step + 2 < ITERS:
                    keep(moment.at[(step + 1) % 2, side], rows, value)
                keep_factor(side, index, rows, value)
    final = root.at[(ITERS - 1) % 2]
    for side in range(2):
        for rows in parts:
            value = product3(held.at[side], factor.at[side], rows)
            roots[side, rows, :] = value
            keep(final.at[side], rows, value)
    for rows in parts:
        keep(mixed, rows, product3(final.at[0], mean, rows))
    for index, rows in enumerate(parts):
        value = product3(mixed, final.at[1], rows)
        value = value.reshape(n_z // 2, plane, width // (n_z * plane), width).astype(BF16)
        for j in range(n_z // 2):
            out[:, index * (n_z // 2) + j] = value[j]


def refresh(near, far, x, q):
    n_micro = lax.axis_size("x")
    n_z, width = len(near), x.shape[-1]
    plane = far.shape[0] // n_micro
    rows = far.shape[2]
    matrix = (2, 2, width, width)
    return pl.pallas_call(
        functools.partial(refresh_kernel, n_z),
        out_shape=(
            jax.ShapeDtypeStruct((2, width, width), F32),
            jax.ShapeDtypeStruct((plane, n_z, rows, width), BF16),
        ),
        in_specs=[VMEM] * (n_z + 3),
        out_specs=(VMEM, VMEM),
        scratch_shapes=[
            pltpu.VMEM((n_micro, width, width), BF16),
            pltpu.VMEM(matrix, BF16),
            pltpu.VMEM((2,) + matrix, BF16),
            pltpu.VMEM(matrix, BF16),
            pltpu.VMEM((2,) + matrix, BF16),
            pltpu.VMEM((2,) + matrix, BF16),
            pltpu.VMEM((2, width, width), BF16),
            pltpu.VMEM((2, width, width), BF16),
        ],
        compiler_params=pltpu.CompilerParams(vmem_limit_bytes=REFRESH_MB * MB),
        cost_estimate=pl.CostEstimate(
            flops=(22 * 3 + 8) * 2 * width**3, bytes_accessed=9 * MB, transcendentals=0
        ),
        name="refresh_roots",
    )(*near, far, x, q)


def sort_kernel(order, local, *outs):
    by_plane, by_shift = outs[0], outs[1:]
    n_z, plane, half = len(by_shift), lax.axis_size("y") * lax.axis_size("c"), by_plane.shape[-1]
    z = lax.axis_index("z")

    def step(i, _):
        first = (i // plane) * (plane * n_z) + lax.rem(i, plane)
        targets = [lax.rem(z + shift, n_z) for shift in range(n_z)]
        values = [local[order[first + target * plane]] for target in targets]
        for target, keeper, value in zip(targets, by_shift, values):
            by_plane[i, target] = value[:, :half]
            keeper[i] = value[:, half:]
        return 0

    lax.fori_loop(0, by_plane.shape[0], step, 0, unroll=4)


def sort_blocks(order, local):
    n_z = lax.axis_size("z")
    count = order.shape[0] // n_z
    rows, width = local.shape[1:]
    piece = jax.ShapeDtypeStruct((count, rows, width // 2), BF16)
    first, *rest = pl.pallas_call(
        sort_kernel,
        out_shape=[jax.ShapeDtypeStruct((count, n_z, rows, width // 2), BF16)] + [piece] * n_z,
        in_specs=[SMEM, VMEM],
        out_specs=[VMEM] * (n_z + 1),
        compiler_params=pltpu.CompilerParams(vmem_limit_bytes=12 * MB),
        cost_estimate=pl.CostEstimate(flops=0, bytes_accessed=4 * MB, transcendentals=0),
        name="sort_blocks",
    )(order, local)
    return first, rest


def cut_kernel(value, *outs):
    n_z = len(outs)
    z = lax.axis_index("z")
    targets = [lax.rem(z + shift, n_z) for shift in range(n_z)]

    def step(i, _):
        held = [value[i, target] for target in targets]
        for out, piece in zip(outs, held):
            out[i] = piece
        return 0

    lax.fori_loop(0, value.shape[0], step, 0, unroll=4)


def cut(value):
    count, n_z, rows, width = value.shape
    return pl.pallas_call(
        cut_kernel,
        out_shape=[jax.ShapeDtypeStruct((count, rows, width), value.dtype)] * n_z,
        in_specs=[VMEM],
        out_specs=[VMEM] * n_z,
        compiler_params=pltpu.CompilerParams(vmem_limit_bytes=8 * MB),
        cost_estimate=pl.CostEstimate(
            flops=0, bytes_accessed=4 * value.size, transcendentals=0
        ),
        name="cut_by_shift",
    )(value)


def stack_kernel(*refs):
    pieces, out = refs[:-1], refs[-1]

    def step(i, _):
        held = [piece[i] for piece in pieces]
        for shift, piece in enumerate(held):
            out[i, shift] = piece
        return 0

    lax.fori_loop(0, out.shape[0], step, 0, unroll=4)


def stack(pieces):
    count, rows, width = pieces[0].shape
    return pl.pallas_call(
        stack_kernel,
        out_shape=jax.ShapeDtypeStruct((count, len(pieces), rows, width), BF16),
        in_specs=[VMEM] * len(pieces),
        out_specs=VMEM,
        compiler_params=pltpu.CompilerParams(vmem_limit_bytes=8 * MB),
        cost_estimate=pl.CostEstimate(flops=0, bytes_accessed=2 * MB, transcendentals=0),
        name="stack_shifts",
    )(*pieces)


def place_kernel(sources, order, *refs):
    pieces, (out, sems) = refs[: len(sources)], refs[-2:]
    n_x, n_z = lax.axis_size("x"), lax.axis_size("z")
    plane = order.shape[0] // (n_x * n_z)
    x, z = lax.axis_index("x"), lax.axis_index("z")
    for number, (piece, (by, shifts)) in enumerate(zip(pieces, sources)):
        for index, shift in enumerate(shifts):
            first = lax.rem(x + by, n_x) * n_z + lax.rem(z + (n_z - shift), n_z)
            for j in range(plane):
                block = order[first * plane + j]
                pltpu.make_async_copy(
                    piece.at[index * plane + j], out.at[block], sems.at[number]
                ).start()
    for number, piece in enumerate(pieces):
        pltpu.make_async_copy(piece, out.at[pl.ds(0, piece.shape[0])], sems.at[number]).wait()


def place(order, pieces, sources, base):
    rows, width = pieces[0].shape[1:]
    count = len(pieces)
    args, specs, aliases = [order, *pieces], [SMEM] + [VMEM] * count, {}
    if base is not None:
        args.append(base)
        specs.append(ANY)
        aliases = {count + 1: 0}
    return pl.pallas_call(
        functools.partial(place_kernel, sources),
        out_shape=jax.ShapeDtypeStruct((order.shape[0], rows, width), BF16),
        in_specs=specs,
        out_specs=ANY,
        scratch_shapes=[pltpu.SemaphoreType.DMA((count,))],
        input_output_aliases=aliases,
        compiler_params=pltpu.CompilerParams(vmem_limit_bytes=8 * MB),
        cost_estimate=pl.CostEstimate(
            flops=0, bytes_accessed=4 * sum(p.size for p in pieces), transcendentals=0
        ),
        name="place_blocks",
    )(*args)


def move(value, axis, by):
    count = lax.axis_size(axis)
    if by % count == 0:
        return value
    return lax.ppermute(value, axis, [(i, (i + by) % count) for i in range(count)])


def by_distance(n_z):
    return sorted(range(n_z), key=lambda shift: -min(shift, n_z - shift))


def after(values, token):
    held = lax.optimization_barrier((tuple(values), token))
    return list(held[0]), held[1]


def body(grads, order, prev_roots):
    n_x, n_z = lax.axis_size("x"), lax.axis_size("z")
    far_first = by_distance(n_z)
    middle = n_z // 2
    early, late = far_first[:middle], far_first[middle:]
    by_plane, by_shift = sort_blocks(order, grads[0])
    far, near = {}, {}
    for shift in early:
        far[shift] = move(by_shift[shift], "z", shift)
    arrived = lax.all_to_all(by_plane, ("x", "y", "c"), split_axis=0, concat_axis=0, tiled=True)
    rest, arrived = after([by_shift[shift] for shift in late], arrived)
    for shift, piece in zip(late, rest):
        far[shift] = move(piece, "z", shift)
    pieces = cut(arrived)
    for shift in early:
        near[shift] = move(pieces[shift], "z", shift)
    stacked = stack([far[shift] for shift in range(n_z)])
    far = lax.all_to_all(stacked, ("x", "y", "c"), split_axis=0, concat_axis=0, tiled=True)
    rest, far = after([pieces[shift] for shift in late], far)
    for shift, piece in zip(late, rest):
        near[shift] = move(piece, "z", shift)
    x, q = fourth_powers(prev_roots[0])
    roots, refreshed = refresh([near[shift] for shift in range(n_z)], far, x, q)
    mine = lax.all_to_all(refreshed, ("y", "c"), split_axis=0, concat_axis=0, tiled=True)
    pieces = cut(mine)
    mine = [move(piece, "z", shift) for shift, piece in enumerate(pieces)]
    batches = [([mine[shift] for shift in range(n_z)], [(0, (shift,)) for shift in range(n_z)])]
    for group in (late, early):
        first, second = tuple(group[: middle // 2]), tuple(group[middle // 2 :])
        low = jnp.concatenate([mine[shift] for shift in first], axis=0)
        high = jnp.concatenate([mine[shift] for shift in second], axis=0)
        low_up, high_down = move(low, "x", 1), move(high, "x", -1)
        high_up, low_down = move(high, "x", 1), move(low, "x", -1)
        low_far, high_far = move(low_up, "x", 1), move(high_down, "x", -1)
        batches[-1][0].extend((low_up, high_down, high_up, low_down))
        batches[-1][1].extend(((n_x - 1, first), (1, second), (n_x - 1, second), (1, first)))
        batches.append(([low_far, high_far], [(n_x - 2, first), (2, second)]))
    result = None
    for pieces, sources in batches:
        result = place(order, pieces, tuple(sources), result)
    return (result, roots[None])


def solution(mesh):
    n_x, n_f = mesh.devices.shape
    fine = Mesh(mesh.devices.reshape(n_x, n_f // 8, 4, 2), ("x", "z", "y", "c"))
    owners = P(("x", "z", "y", "c"), None, None, None)
    return jax.shard_map(
        body,
        mesh=fine,
        in_specs=(P("x", None, ("z", "y", "c"), None), P(), owners),
        out_specs=(P(None, ("z", "y", "c"), None), owners),
        check_vma=False,
    )
```

```python
import functools

import jax
import jax.numpy as jnp
from jax import lax
from jax.experimental import pallas as pl
from jax.experimental.pallas import tpu as pltpu
from jax.sharding import PartitionSpec as P

ITERS = 3
MB = 1 << 20
BF16 = jnp.bfloat16
F32 = jnp.float32
ANY = pl.BlockSpec(memory_space=pl.ANY)
VMEM = pl.BlockSpec(memory_space=pltpu.VMEM)
SMEM = pl.BlockSpec(memory_space=pltpu.SMEM)


def split(value):
    high = value.astype(BF16)
    return high, (value - high.astype(F32)).astype(BF16)


def product3(lhs, rhs, rows):
    high = lhs[0, rows, :]
    left = jnp.concatenate([high, lhs[1, rows, :], high], axis=1)
    over = rhs[0]
    right = jnp.concatenate([over, over, rhs[1]], axis=0)
    return jnp.dot(left, right, preferred_element_type=F32)


def keep(target, rows, value):
    high, low = split(value)
    target[0, rows, :] = high
    target[1, rows, :] = low


def halves(width):
    size = width // 2
    return [pl.ds(0, size), pl.ds(size, size)]


def fourth_kernel(prev, x_out, q_out, square):
    width = prev.shape[-1]
    for side in range(2):
        keep(x_out.at[side], slice(None), prev[side])
    for source, target in ((x_out, square), (square, q_out)):
        for rows in halves(width):
            for side in range(2):
                keep(target.at[side], rows, product3(source.at[side], source.at[side], rows))


def fourth_powers(prev):
    width = prev.shape[-1]
    pair = jax.ShapeDtypeStruct((2, 2, width, width), BF16)
    return pl.pallas_call(
        fourth_kernel,
        out_shape=(pair, pair),
        in_specs=[VMEM],
        out_specs=(VMEM, VMEM),
        scratch_shapes=[pltpu.VMEM((2, 2, width, width), BF16)],
        compiler_params=pltpu.CompilerParams(vmem_limit_bytes=20 * MB),
        cost_estimate=pl.CostEstimate(
            flops=2 * 2 * 3 * 2 * width**3, bytes_accessed=6 * MB, transcendentals=0
        ),
        name="fourth_powers",
    )(prev)


def refresh_kernel(
    arrived, x, q, roots, out,
    grads, partial, stat, moment, factor, power, root, final, mean, mixed, sems,
):
    n_micro, width = grads.shape[0], grads.shape[-1]
    parts = halves(width)
    size = width // 2
    batches = [pl.ds(0, n_micro // 2), pl.ds(n_micro // 2, n_micro // 2)]
    copies = [
        pltpu.make_async_copy(arrived.at[batch], grads.at[batch], sems.at[number])
        for number, batch in enumerate(batches)
    ]
    for copy in copies:
        copy.start()
    contracts = ((((1,), (1,)), ((), ())), (((0,), (0,)), ((), ())))
    totals = [jnp.zeros((1, 1), F32), jnp.zeros((1, 1), F32)]
    for number, copy in enumerate(copies):
        copy.wait()
        first = number * (n_micro // 2)
        whole = [grads[d] for d in range(first, first + n_micro // 2)]
        for side in range(2):
            rhs = jnp.concatenate(whole, axis=1 - side)
            for index, rows in enumerate(parts):
                lo, hi = index * size, (index + 1) * size
                lhs = rhs[lo:hi, :] if side == 0 else rhs[:, lo:hi]
                value = lax.dot_general(lhs, rhs, contracts[side], preferred_element_type=F32)
                if number == 0:
                    partial[side, rows, :] = value
                else:
                    value = value + partial[side, rows, :]
                    totals[side] = totals[side] + jnp.sum(
                        value * value, axis=(0, 1), keepdims=True
                    )
                    keep(stat.at[side], rows, value)
    scales = [1.0 / (jnp.sqrt(total / (width * width) + 1e-06) * width) for total in totals]

    row_ids = lax.broadcasted_iota(jnp.int32, (size, width), 0)
    col_ids = lax.broadcasted_iota(jnp.int32, (size, width), 1)

    def keep_factor(side, index, rows, value):
        diagonal = jnp.where(row_ids + index * size == col_ids, 1.25, 0.0)
        keep(factor.at[side], rows, diagonal - 0.25 * value)

    for side in range(2):
        for index, rows in enumerate(parts):
            value = product3(q.at[side], stat.at[side], rows) * scales[side]
            keep(moment.at[0, side], rows, value)
            keep_factor(side, index, rows, value)
    for index, rows in enumerate(parts):
        value = grads[0, rows, :].astype(F32)
        for d in range(1, n_micro):
            value = value + grads[d, rows, :].astype(F32)
        keep(mean, rows, value / n_micro)
    held = x
    for step in range(ITERS - 1):
        for side in range(2):
            for rows in parts:
                keep(
                    power.at[0, side], rows, product3(factor.at[side], factor.at[side], rows)
                )
        for side in range(2):
            for rows in parts:
                keep(
                    power.at[1, side],
                    rows,
                    product3(power.at[0, side], power.at[0, side], rows),
                )
        for side in range(2):
            for rows in parts:
                keep(
                    root.at[step % 2, side], rows, product3(held.at[side], factor.at[side], rows)
                )
        held = root.at[step % 2]
        for side in range(2):
            for index, rows in enumerate(parts):
                value = product3(power.at[1, side], moment.at[step % 2, side], rows)
                if step + 2 < ITERS:
                    keep(moment.at[(step + 1) % 2, side], rows, value)
                keep_factor(side, index, rows, value)
    last = root.at[(ITERS - 1) % 2]
    writes = []
    for side in range(2):
        for rows in parts:
            value = product3(held.at[side], factor.at[side], rows)
            final[side, rows, :] = value
            keep(last.at[side], rows, value)
        write = pltpu.make_async_copy(final.at[side], roots.at[side], sems.at[side])
        write.start()
        writes.append(write)
    for rows in parts:
        keep(mixed, rows, product3(last.at[0], mean, rows))
    for rows in parts:
        out[rows, :] = product3(mixed, last.at[1], rows).astype(BF16)
    for write in writes:
        write.wait()


def refresh(arrived, x, q):
    n_micro, width = arrived.shape[0], arrived.shape[-1]
    matrix = (2, 2, width, width)
    return pl.pallas_call(
        refresh_kernel,
        out_shape=(
            jax.ShapeDtypeStruct((2, width, width), F32),
            jax.ShapeDtypeStruct((width, width), BF16),
        ),
        in_specs=[ANY, VMEM, VMEM],
        out_specs=(ANY, VMEM),
        scratch_shapes=[
            pltpu.VMEM((n_micro, width, width), BF16),
            pltpu.VMEM((2, width, width), F32),
            pltpu.VMEM(matrix, BF16),
            pltpu.VMEM((2,) + matrix, BF16),
            pltpu.VMEM(matrix, BF16),
            pltpu.VMEM((2,) + matrix, BF16),
            pltpu.VMEM((2,) + matrix, BF16),
            pltpu.VMEM((2, width, width), F32),
            pltpu.VMEM((2, width, width), BF16),
            pltpu.VMEM((2, width, width), BF16),
            pltpu.SemaphoreType.DMA((2,)),
        ],
        compiler_params=pltpu.CompilerParams(vmem_limit_bytes=30 * MB),
        cost_estimate=pl.CostEstimate(
            flops=(22 * 3 + 8) * 2 * width**3, bytes_accessed=9 * MB, transcendentals=0
        ),
        name="refresh_roots",
    )(arrived, x, q)


def place_kernel(owners, offsets, order, *refs):
    pieces, (out, sems) = refs[: len(offsets)], refs[-2:]
    n_data, mine = lax.axis_size("dp"), lax.axis_index("dp")
    for number, (piece, (by, skip)) in enumerate(zip(pieces, offsets)):
        base = lax.rem(mine + by, n_data) * owners + skip
        for i in range(piece.shape[0]):
            pltpu.make_async_copy(
                piece.at[i], out.at[order[base + i]], sems.at[number]
            ).start()
    for number, piece in enumerate(pieces):
        pltpu.make_async_copy(piece, out.at[pl.ds(0, piece.shape[0])], sems.at[number]).wait()


def place(owners, order, batch, base):
    offsets, pieces = zip(*batch)
    rows, width = pieces[0].shape[1:]
    count = len(pieces)
    args, specs, aliases = [order, *pieces], [SMEM] + [VMEM] * count, {}
    if base is not None:
        args.append(base)
        specs.append(ANY)
        aliases = {count + 1: 0}
    return pl.pallas_call(
        functools.partial(place_kernel, owners, offsets),
        out_shape=jax.ShapeDtypeStruct((order.shape[0], rows, width), BF16),
        in_specs=specs,
        out_specs=ANY,
        scratch_shapes=[pltpu.SemaphoreType.DMA((count,))],
        input_output_aliases=aliases,
        compiler_params=pltpu.CompilerParams(vmem_limit_bytes=8 * MB),
        cost_estimate=pl.CostEstimate(
            flops=0, bytes_accessed=4 * sum(p.size for p in pieces), transcendentals=0
        ),
        name="place_blocks",
    )(*args)


def body(grads, order, prev_roots):
    n_data = lax.axis_size("dp")
    local = grads[0]
    rows, width = local.shape[1:]
    outgoing = local.at[order].get(
        mode="promise_in_bounds", unique_indices=True, wrap_negative_indices=False
    )
    arrived = lax.all_to_all(outgoing, ("dp", "fsdp"), split_axis=0, concat_axis=0, tiled=True)
    x, q = fourth_powers(prev_roots[0])
    roots, refreshed = refresh(arrived.reshape(n_data, width, width), x, q)
    pieces = refreshed.reshape(width // rows, rows, width)
    mine = lax.all_to_all(pieces, "fsdp", split_axis=0, concat_axis=0, tiled=True)
    owners = mine.shape[0]
    half = owners // 2

    def shift(value, by):
        return lax.ppermute(value, "dp", [(i, (i + by) % n_data) for i in range(n_data)])

    low, high = mine[:half], mine[half:]
    low_up, high_down = shift(low, 1), shift(high, -1)
    high_up, low_down = shift(high, 1), shift(low, -1)
    low_far, high_far = shift(low_up, 1), shift(high_down, -1)
    result = None
    for batch in (
        (((0, 0), mine), ((n_data - 1, 0), low_up), ((1, half), high_down)),
        (((n_data - 1, half), high_up), ((1, 0), low_down)),
        (((n_data - 2, 0), low_far), ((2, half), high_far)),
    ):
        result = place(owners, order, batch, result)
    return (result, roots[None])


def solution(mesh):
    return jax.shard_map(
        body,
        mesh=mesh,
        in_specs=(P("dp", None, "fsdp", None), P(), P(("dp", "fsdp"), None, None, None)),
        out_specs=(P(None, "fsdp", None), P(("dp", "fsdp"), None, None, None)),
        check_vma=False,
    )
```

```python
import functools

import jax
import jax.numpy as jnp
from jax import lax
from jax.experimental import pallas as pl
from jax.experimental.pallas import tpu as pltpu
from jax.sharding import PartitionSpec as P

MB = 1 << 20
PARTS = 2
BF16 = jnp.bfloat16
F32 = jnp.float32
ANY = pl.BlockSpec(memory_space=pl.ANY)
VMEM = pl.BlockSpec(memory_space=pltpu.VMEM)
SMEM = pl.BlockSpec(memory_space=pltpu.SMEM)


def split(value):
    high = value.astype(BF16)
    return high, (value - high.astype(F32)).astype(BF16)


def product3(lhs, rhs, rows):
    high = lhs[0, rows, :]
    left = jnp.concatenate([high, lhs[1, rows, :], high], axis=1)
    over = rhs[0]
    right = jnp.concatenate([over, over, rhs[1]], axis=0)
    return jnp.dot(left, right, preferred_element_type=F32)


def keep(target, rows, value):
    high, low = split(value)
    target[0, rows, :] = high
    target[1, rows, :] = low


def cut(width, count):
    size = width // count
    return [pl.ds(index * size, size) for index in range(count)]


def fourth_kernel(prev, out, square):
    x_out, q_out = out.at[0], out.at[1]
    width = prev.shape[-1]
    for side in range(2):
        keep(x_out.at[side], slice(None), prev[side])
    for source, target in ((x_out, square), (square, q_out)):
        for side in range(2):
            for rows in cut(width, PARTS):
                keep(target.at[side], rows, product3(source.at[side], source.at[side], rows))


def fourth_powers(prev):
    width = prev.shape[-1]
    return pl.pallas_call(
        fourth_kernel,
        out_shape=jax.ShapeDtypeStruct((2, 2, 2, width, width), BF16),
        in_specs=[VMEM],
        out_specs=VMEM,
        scratch_shapes=[pltpu.VMEM((2, 2, width, width), BF16)],
        compiler_params=pltpu.CompilerParams(vmem_limit_bytes=20 * MB),
        cost_estimate=pl.CostEstimate(
            flops=2 * 2 * 3 * 2 * width**3, bytes_accessed=6 * MB, transcendentals=0
        ),
        name="fourth_powers",
    )(prev)


def refresh_kernel(
    arrived, powers, roots, out,
    grads, x, q, stat, moment, factor, power, root, final, mean, mixed, sems,
):
    n_micro, width = grads.shape[0], grads.shape[-1]
    parts = cut(width, PARTS)
    size = width // PARTS
    batches = [pl.ds(0, n_micro // 2), pl.ds(n_micro // 2, n_micro // 2)]
    copies = [
        pltpu.make_async_copy(arrived.at[batch], grads.at[batch], sems.at[number])
        for number, batch in enumerate(batches)
    ]
    loads = [
        pltpu.make_async_copy(powers.at[1], q, sems.at[2]),
        pltpu.make_async_copy(powers.at[0], x, sems.at[3]),
    ]
    for copy in copies + loads:
        copy.start()
    for copy in copies:
        copy.wait()
    contracts = ((((1,), (1,)), ((), ())), (((0,), (0,)), ((), ())))
    scales = []
    whole = [grads[d] for d in range(n_micro)]
    for side in range(2):
        total = jnp.zeros((1, 1), F32)
        rhs = jnp.concatenate(whole, axis=1 - side)
        for index, rows in enumerate(parts):
            lo, hi = index * size, (index + 1) * size
            lhs = rhs[lo:hi, :] if side == 0 else rhs[:, lo:hi]
            value = lax.dot_general(lhs, rhs, contracts[side], preferred_element_type=F32)
            total = total + jnp.sum(value * value, axis=(0, 1), keepdims=True)
            keep(stat.at[side], rows, value)
        scales.append(1.0 / (jnp.sqrt(total / (width * width) + 1e-06) * width))

    row_ids = lax.broadcasted_iota(jnp.int32, (size, width), 0)
    col_ids = lax.broadcasted_iota(jnp.int32, (size, width), 1)

    def keep_factor(side, index, rows, value):
        diagonal = jnp.where(row_ids + index * size == col_ids, 1.25, 0.0)
        keep(factor.at[side], rows, diagonal - 0.25 * value)

    def five_quarters(side, rows):
        return 1.25 * (factor[side, 0, rows, :].astype(F32) + factor[side, 1, rows, :].astype(F32))

    for index, rows in enumerate(parts):
        value = grads[0, rows, :].astype(F32)
        for d in range(1, n_micro):
            value = value + grads[d, rows, :].astype(F32)
        keep(mean, rows, value / n_micro)
    for copy in loads:
        copy.wait()
    for index, rows in enumerate(parts):
        for side in range(2):
            value = product3(q.at[side], stat.at[side], rows) * scales[side]
            keep(moment.at[side], rows, value)
            keep_factor(side, index, rows, value)
    for rows in parts:
        for side in range(2):
            keep(power.at[0, side], rows, product3(factor.at[side], factor.at[side], rows))
    for rows in parts:
        for side in range(2):
            keep(root.at[side], rows, product3(x.at[side], factor.at[side], rows))
    for rows in parts:
        for side in range(2):
            keep(power.at[1, side], rows, product3(power.at[0, side], power.at[0, side], rows))
    for index, rows in enumerate(parts):
        for side in range(2):
            keep_factor(side, index, rows, product3(power.at[1, side], moment.at[side], rows))
    for rows in parts:
        for side in range(2):
            value = product3(factor.at[side], factor.at[side], rows)
            keep(power.at[0, side], rows, value)
            keep(power.at[1, side], rows, value - five_quarters(side, rows))
    for rows in parts:
        for side in range(2):
            keep(moment.at[side], rows, product3(power.at[0, side], power.at[1, side], rows))
    for rows in parts:
        for side in range(2):
            value = product3(power.at[0, side], moment.at[side], rows)
            keep(stat.at[side], rows, value + five_quarters(side, rows))
    last = power.at[1]
    writes = []
    for side in range(2):
        for rows in parts:
            value = product3(root.at[side], stat.at[side], rows)
            final[side, rows, :] = value
            keep(last.at[side], rows, value)
        write = pltpu.make_async_copy(final.at[side], roots.at[side], sems.at[side])
        write.start()
        writes.append(write)
    for rows in cut(width, 2):
        keep(mixed, rows, product3(last.at[0], mean, rows))
    for rows in cut(width, 2):
        out[rows, :] = product3(mixed, last.at[1], rows).astype(BF16)
    for write in writes:
        write.wait()


def refresh(arrived, powers):
    n_micro, width = arrived.shape[0], arrived.shape[-1]
    matrix = (2, 2, width, width)
    return pl.pallas_call(
        refresh_kernel,
        out_shape=(
            jax.ShapeDtypeStruct((2, width, width), F32),
            jax.ShapeDtypeStruct((width, width), BF16),
        ),
        in_specs=[ANY, ANY],
        out_specs=(ANY, VMEM),
        scratch_shapes=[
            pltpu.VMEM((n_micro, width, width), BF16),
            pltpu.VMEM(matrix, BF16),
            pltpu.VMEM(matrix, BF16),
            pltpu.VMEM(matrix, BF16),
            pltpu.VMEM(matrix, BF16),
            pltpu.VMEM(matrix, BF16),
            pltpu.VMEM((2,) + matrix, BF16),
            pltpu.VMEM(matrix, BF16),
            pltpu.VMEM((2, width, width), F32),
            pltpu.VMEM((2, width, width), BF16),
            pltpu.VMEM((2, width, width), BF16),
            pltpu.SemaphoreType.DMA((4,)),
        ],
        compiler_params=pltpu.CompilerParams(vmem_limit_bytes=59 * MB),
        cost_estimate=pl.CostEstimate(
            flops=(20 * 3 + 8) * 2 * width**3, bytes_accessed=9 * MB, transcendentals=0
        ),
        name="refresh_roots",
    )(arrived, powers)


def place_kernel(owners, offsets, order, *refs):
    pieces, (out, sems) = refs[: len(offsets)], refs[-2:]
    n_data, mine = lax.axis_size("dp"), lax.axis_index("dp")
    for number, (piece, (by, skip)) in enumerate(zip(pieces, offsets)):
        base = lax.rem(mine + by, n_data) * owners + skip
        for i in range(piece.shape[0]):
            pltpu.make_async_copy(
                piece.at[i], out.at[order[base + i]], sems.at[number]
            ).start()
    for number, piece in enumerate(pieces):
        pltpu.make_async_copy(piece, out.at[pl.ds(0, piece.shape[0])], sems.at[number]).wait()


def place(owners, order, batch, base):
    offsets, pieces = zip(*batch)
    rows, width = pieces[0].shape[1:]
    count = len(pieces)
    args, specs, aliases = [order, *pieces], [SMEM] + [VMEM] * count, {}
    if base is not None:
        args.append(base)
        specs.append(ANY)
        aliases = {count + 1: 0}
    return pl.pallas_call(
        functools.partial(place_kernel, owners, offsets),
        out_shape=jax.ShapeDtypeStruct((order.shape[0], rows, width), BF16),
        in_specs=specs,
        out_specs=ANY,
        scratch_shapes=[pltpu.SemaphoreType.DMA((count,))],
        input_output_aliases=aliases,
        compiler_params=pltpu.CompilerParams(vmem_limit_bytes=8 * MB),
        cost_estimate=pl.CostEstimate(
            flops=0, bytes_accessed=4 * sum(p.size for p in pieces), transcendentals=0
        ),
        name="place_blocks",
    )(*args)


def body(grads, order, prev_roots):
    n_data = lax.axis_size("dp")
    local = grads[0]
    rows, width = local.shape[1:]
    outgoing = local.at[order].get(
        mode="promise_in_bounds", unique_indices=True, wrap_negative_indices=False
    )
    arrived = lax.all_to_all(outgoing, ("dp", "fsdp"), split_axis=0, concat_axis=0, tiled=True)
    powers = fourth_powers(prev_roots[0])
    roots, refreshed = refresh(arrived.reshape(n_data, width, width), powers)
    pieces = refreshed.reshape(width // rows, rows, width)
    mine = lax.all_to_all(pieces, "fsdp", split_axis=0, concat_axis=0, tiled=True)
    owners = mine.shape[0]
    half = owners // 2

    def shift(value, by):
        return lax.ppermute(value, "dp", [(i, (i + by) % n_data) for i in range(n_data)])

    low, high = mine[:half], mine[half:]
    low_up, high_down = shift(low, 1), shift(high, -1)
    high_up, low_down = shift(high, 1), shift(low, -1)
    low_far, high_far = shift(low_up, 1), shift(high_down, -1)
    result = None
    for batch in (
        (((0, 0), mine), ((n_data - 1, 0), low_up), ((1, half), high_down)),
        (((n_data - 1, half), high_up), ((1, 0), low_down)),
        (((n_data - 2, 0), low_far), ((2, half), high_far)),
    ):
        result = place(owners, order, batch, result)
    return (result, roots[None])


def solution(mesh):
    return jax.shard_map(
        body,
        mesh=mesh,
        in_specs=(P("dp", None, "fsdp", None), P(), P(("dp", "fsdp"), None, None, None)),
        out_specs=(P(None, "fsdp", None), P(("dp", "fsdp"), None, None, None)),
        check_vma=False,
    )
```

```python
import functools

import jax
import jax.numpy as jnp
from jax import lax
from jax.experimental import pallas as pl
from jax.experimental.pallas import tpu as pltpu
from jax.sharding import PartitionSpec as P

MB = 1 << 20
PARTS = 2
BF16 = jnp.bfloat16
F32 = jnp.float32
ANY = pl.BlockSpec(memory_space=pl.ANY)
VMEM = pl.BlockSpec(memory_space=pltpu.VMEM)
SMEM = pl.BlockSpec(memory_space=pltpu.SMEM)


def split(value):
    high = value.astype(BF16)
    return high, (value - high.astype(F32)).astype(BF16)


def product3(lhs, rhs, rows):
    high = lhs[0, rows, :]
    left = jnp.concatenate([high, lhs[1, rows, :], high], axis=1)
    over = rhs[0]
    right = jnp.concatenate([over, over, rhs[1]], axis=0)
    return jnp.dot(left, right, preferred_element_type=F32)


def keep(target, rows, value):
    high, low = split(value)
    target[0, rows, :] = high
    target[1, rows, :] = low


def cut(width, count):
    size = width // count
    return [pl.ds(index * size, size) for index in range(count)]


def fourth_kernel(prev, out, square):
    x_out, q_out = out.at[0], out.at[1]
    width = prev.shape[-1]
    for side in range(2):
        keep(x_out.at[side], slice(None), prev[side])
    for source, target in ((x_out, square), (square, q_out)):
        for side in range(2):
            for rows in cut(width, PARTS):
                keep(target.at[side], rows, product3(source.at[side], source.at[side], rows))


def fourth_powers(prev):
    width = prev.shape[-1]
    return pl.pallas_call(
        fourth_kernel,
        out_shape=jax.ShapeDtypeStruct((2, 2, 2, width, width), BF16),
        in_specs=[VMEM],
        out_specs=VMEM,
        scratch_shapes=[pltpu.VMEM((2, 2, width, width), BF16)],
        compiler_params=pltpu.CompilerParams(vmem_limit_bytes=20 * MB),
        cost_estimate=pl.CostEstimate(
            flops=2 * 2 * 3 * 2 * width**3, bytes_accessed=6 * MB, transcendentals=0
        ),
        name="fourth_powers",
    )(prev)


def refresh_kernel(
    arrived, powers, roots, out,
    grads, x, q, stat, moment, factor, power, root, final, mean, mixed, sems,
):
    n_micro, width = grads.shape[0], grads.shape[-1]
    parts = cut(width, PARTS)
    size = width // PARTS
    copies = [
        pltpu.make_async_copy(arrived.at[d], grads.at[d], sems.at[d]) for d in range(n_micro)
    ]
    loads = [
        pltpu.make_async_copy(powers.at[1], q, sems.at[n_micro]),
        pltpu.make_async_copy(powers.at[0], x, sems.at[n_micro + 1]),
    ]
    for copy in copies:
        copy.start()
    for copy in copies:
        copy.wait()
    for copy in loads:
        copy.start()
    contracts = ((((1,), (1,)), ((), ())), (((0,), (0,)), ((), ())))
    scales = []
    whole = [grads[d] for d in range(n_micro)]
    for side in range(2):
        total = jnp.zeros((1, 1), F32)
        rhs = jnp.concatenate(whole, axis=1 - side)
        for index, rows in enumerate(parts):
            lo, hi = index * size, (index + 1) * size
            lhs = rhs[lo:hi, :] if side == 0 else rhs[:, lo:hi]
            value = lax.dot_general(lhs, rhs, contracts[side], preferred_element_type=F32)
            total = total + jnp.sum(value * value, axis=(0, 1), keepdims=True)
            keep(stat.at[side], rows, value)
        scales.append(1.0 / (jnp.sqrt(total / (width * width) + 1e-06) * width))

    row_ids = lax.broadcasted_iota(jnp.int32, (size, width), 0)
    col_ids = lax.broadcasted_iota(jnp.int32, (size, width), 1)

    def keep_factor(side, index, rows, value):
        diagonal = jnp.where(row_ids + index * size == col_ids, 1.25, 0.0)
        keep(factor.at[side], rows, diagonal - 0.25 * value)

    def five_quarters(side, rows):
        return 1.25 * (factor[side, 0, rows, :].astype(F32) + factor[side, 1, rows, :].astype(F32))

    for index, rows in enumerate(parts):
        value = grads[0, rows, :].astype(F32)
        for d in range(1, n_micro):
            value = value + grads[d, rows, :].astype(F32)
        keep(mean, rows, value / n_micro)
    loads[0].wait()
    for index, rows in enumerate(parts):
        for side in range(2):
            value = product3(q.at[side], stat.at[side], rows) * scales[side]
            keep(moment.at[side], rows, value)
            keep_factor(side, index, rows, value)
    for rows in parts:
        for side in range(2):
            keep(power.at[0, side], rows, product3(factor.at[side], factor.at[side], rows))
    loads[1].wait()
    for rows in parts:
        for side in range(2):
            keep(root.at[side], rows, product3(x.at[side], factor.at[side], rows))
    for rows in parts:
        for side in range(2):
            keep(power.at[1, side], rows, product3(power.at[0, side], power.at[0, side], rows))
    for index, rows in enumerate(parts):
        for side in range(2):
            keep_factor(side, index, rows, product3(power.at[1, side], moment.at[side], rows))
    for rows in parts:
        for side in range(2):
            value = product3(factor.at[side], factor.at[side], rows)
            keep(power.at[0, side], rows, value)
            keep(power.at[1, side], rows, value - five_quarters(side, rows))
    for rows in parts:
        for side in range(2):
            keep(moment.at[side], rows, product3(power.at[0, side], power.at[1, side], rows))
    for rows in parts:
        for side in range(2):
            value = product3(power.at[0, side], moment.at[side], rows)
            keep(stat.at[side], rows, value + five_quarters(side, rows))
    last = power.at[1]
    writes = []
    for side in range(2):
        for rows in parts:
            value = product3(root.at[side], stat.at[side], rows)
            final[side, rows, :] = value
            keep(last.at[side], rows, value)
        write = pltpu.make_async_copy(final.at[side], roots.at[side], sems.at[side])
        write.start()
        writes.append(write)
    for rows in cut(width, 2):
        keep(mixed, rows, product3(last.at[0], mean, rows))
    for rows in cut(width, 2):
        out[rows, :] = product3(mixed, last.at[1], rows).astype(BF16)
    for write in writes:
        write.wait()


def refresh(arrived, powers):
    n_micro, width = arrived.shape[0], arrived.shape[-1]
    matrix = (2, 2, width, width)
    return pl.pallas_call(
        refresh_kernel,
        out_shape=(
            jax.ShapeDtypeStruct((2, width, width), F32),
            jax.ShapeDtypeStruct((width, width), BF16),
        ),
        in_specs=[ANY, ANY],
        out_specs=(ANY, VMEM),
        scratch_shapes=[
            pltpu.VMEM((n_micro, width, width), BF16),
            pltpu.VMEM(matrix, BF16),
            pltpu.VMEM(matrix, BF16),
            pltpu.VMEM(matrix, BF16),
            pltpu.VMEM(matrix, BF16),
            pltpu.VMEM(matrix, BF16),
            pltpu.VMEM((2,) + matrix, BF16),
            pltpu.VMEM(matrix, BF16),
            pltpu.VMEM((2, width, width), F32),
            pltpu.VMEM((2, width, width), BF16),
            pltpu.VMEM((2, width, width), BF16),
            pltpu.SemaphoreType.DMA((n_micro + 2,)),
        ],
        compiler_params=pltpu.CompilerParams(vmem_limit_bytes=53 * MB),
        cost_estimate=pl.CostEstimate(
            flops=(20 * 3 + 8) * 2 * width**3, bytes_accessed=9 * MB, transcendentals=0
        ),
        name="refresh_roots",
    )(arrived, powers)


def place_kernel(owners, offsets, order, *refs):
    pieces, (out, sems) = refs[: len(offsets)], refs[-2:]
    n_data, mine = lax.axis_size("dp"), lax.axis_index("dp")
    for number, (piece, (by, skip)) in enumerate(zip(pieces, offsets)):
        base = lax.rem(mine + by, n_data) * owners + skip
        for i in range(piece.shape[0]):
            pltpu.make_async_copy(
                piece.at[i], out.at[order[base + i]], sems.at[number]
            ).start()
    for number, piece in enumerate(pieces):
        pltpu.make_async_copy(piece, out.at[pl.ds(0, piece.shape[0])], sems.at[number]).wait()


def place(owners, order, batch, base):
    offsets, pieces = zip(*batch)
    rows, width = pieces[0].shape[1:]
    count = len(pieces)
    args, specs, aliases = [order, *pieces], [SMEM] + [VMEM] * count, {}
    if base is not None:
        args.append(base)
        specs.append(ANY)
        aliases = {count + 1: 0}
    return pl.pallas_call(
        functools.partial(place_kernel, owners, offsets),
        out_shape=jax.ShapeDtypeStruct((order.shape[0], rows, width), BF16),
        in_specs=specs,
        out_specs=ANY,
        scratch_shapes=[pltpu.SemaphoreType.DMA((count,))],
        input_output_aliases=aliases,
        compiler_params=pltpu.CompilerParams(vmem_limit_bytes=8 * MB),
        cost_estimate=pl.CostEstimate(
            flops=0, bytes_accessed=4 * sum(p.size for p in pieces), transcendentals=0
        ),
        name="place_blocks",
    )(*args)


def body(grads, order, prev_roots):
    n_data = lax.axis_size("dp")
    local = grads[0]
    rows, width = local.shape[1:]
    outgoing = local.at[order].get(
        mode="promise_in_bounds", unique_indices=True, wrap_negative_indices=False
    )
    arrived = lax.all_to_all(outgoing, ("dp", "fsdp"), split_axis=0, concat_axis=0, tiled=True)
    powers = fourth_powers(prev_roots[0])
    roots, refreshed = refresh(arrived.reshape(n_data, width, width), powers)
    pieces = refreshed.reshape(width // rows, rows, width)
    mine = lax.all_to_all(pieces, "fsdp", split_axis=0, concat_axis=0, tiled=True)
    owners = mine.shape[0]
    half = owners // 2

    def shift(value, by):
        return lax.ppermute(value, "dp", [(i, (i + by) % n_data) for i in range(n_data)])

    low, high = mine[:half], mine[half:]
    low_up, high_down = shift(low, 1), shift(high, -1)
    high_up, low_down = shift(high, 1), shift(low, -1)
    low_far, high_far = shift(low_up, 1), shift(high_down, -1)
    result = None
    for batch in (
        (((0, 0), mine), ((n_data - 1, 0), low_up), ((1, half), high_down)),
        (((n_data - 1, half), high_up), ((1, 0), low_down)),
        (((n_data - 2, 0), low_far), ((2, half), high_far)),
    ):
        result = place(owners, order, batch, result)
    return (result, roots[None])


def solution(mesh):
    return jax.shard_map(
        body,
        mesh=mesh,
        in_specs=(P("dp", None, "fsdp", None), P(), P(("dp", "fsdp"), None, None, None)),
        out_specs=(P(None, "fsdp", None), P(("dp", "fsdp"), None, None, None)),
        check_vma=False,
    )
```

```python
import functools

import jax
import jax.numpy as jnp
from jax import lax
from jax.experimental import pallas as pl
from jax.experimental.pallas import tpu as pltpu
from jax.sharding import PartitionSpec as P

MB = 1 << 20
PARTS = 1
BF16 = jnp.bfloat16
F32 = jnp.float32
ANY = pl.BlockSpec(memory_space=pl.ANY)
VMEM = pl.BlockSpec(memory_space=pltpu.VMEM)
SMEM = pl.BlockSpec(memory_space=pltpu.SMEM)


def split(value):
    high = value.astype(BF16)
    return high, (value - high.astype(F32)).astype(BF16)


def product3(lhs, rhs, rows):
    high = lhs[0, rows, :]
    left = jnp.concatenate([high, lhs[1, rows, :], high], axis=1)
    over = rhs[0]
    right = jnp.concatenate([over, over, rhs[1]], axis=0)
    return jnp.dot(left, right, preferred_element_type=F32)


def keep(target, rows, value):
    high, low = split(value)
    target[0, rows, :] = high
    target[1, rows, :] = low


def cut(width, count):
    size = width // count
    return [pl.ds(index * size, size) for index in range(count)]


def fourth_kernel(prev, out, square):
    x_out, q_out = out.at[0], out.at[1]
    width = prev.shape[-1]
    for side in range(2):
        keep(x_out.at[side], slice(None), prev[side])
    for source, target in ((x_out, square), (square, q_out)):
        for side in range(2):
            for rows in cut(width, PARTS):
                keep(target.at[side], rows, product3(source.at[side], source.at[side], rows))


def fourth_powers(prev):
    width = prev.shape[-1]
    return pl.pallas_call(
        fourth_kernel,
        out_shape=jax.ShapeDtypeStruct((2, 2, 2, width, width), BF16),
        in_specs=[VMEM],
        out_specs=VMEM,
        scratch_shapes=[pltpu.VMEM((2, 2, width, width), BF16)],
        compiler_params=pltpu.CompilerParams(vmem_limit_bytes=20 * MB),
        cost_estimate=pl.CostEstimate(
            flops=2 * 2 * 3 * 2 * width**3, bytes_accessed=6 * MB, transcendentals=0
        ),
        name="fourth_powers",
    )(prev)


def refresh_kernel(
    arrived, powers, roots, out,
    grads, x, q, stat, moment, factor, power, root, final, mean, mixed, sems,
):
    n_micro, width = grads.shape[0], grads.shape[-1]
    parts = cut(width, PARTS)
    size = width // PARTS
    copies = [
        pltpu.make_async_copy(arrived.at[d], grads.at[d], sems.at[d]) for d in range(n_micro)
    ]
    loads = [
        pltpu.make_async_copy(powers.at[1], q, sems.at[n_micro]),
        pltpu.make_async_copy(powers.at[0], x, sems.at[n_micro + 1]),
    ]
    for copy in copies:
        copy.start()
    for copy in copies:
        copy.wait()
    for copy in loads:
        copy.start()
    contracts = ((((1,), (1,)), ((), ())), (((0,), (0,)), ((), ())))
    scales = []
    whole = [grads[d] for d in range(n_micro)]
    for side in range(2):
        total = jnp.zeros((1, 1), F32)
        rhs = jnp.concatenate(whole, axis=1 - side)
        for index, rows in enumerate(parts):
            lo, hi = index * size, (index + 1) * size
            lhs = rhs[lo:hi, :] if side == 0 else rhs[:, lo:hi]
            value = lax.dot_general(lhs, rhs, contracts[side], preferred_element_type=F32)
            total = total + jnp.sum(value * value, axis=(0, 1), keepdims=True)
            keep(stat.at[side], rows, value)
        scales.append(1.0 / (jnp.sqrt(total / (width * width) + 1e-06) * width))

    row_ids = lax.broadcasted_iota(jnp.int32, (size, width), 0)
    col_ids = lax.broadcasted_iota(jnp.int32, (size, width), 1)

    def keep_factor(side, index, rows, value):
        diagonal = jnp.where(row_ids + index * size == col_ids, 1.25, 0.0)
        keep(factor.at[side], rows, diagonal - 0.25 * value)

    def five_quarters(side, rows):
        return 1.25 * (factor[side, 0, rows, :].astype(F32) + factor[side, 1, rows, :].astype(F32))

    for index, rows in enumerate(parts):
        value = grads[0, rows, :].astype(F32)
        for d in range(1, n_micro):
            value = value + grads[d, rows, :].astype(F32)
        keep(mean, rows, value / n_micro)
    for copy in loads:
        copy.wait()
    for index, rows in enumerate(parts):
        for side in range(2):
            value = product3(q.at[side], stat.at[side], rows) * scales[side]
            keep(moment.at[side], rows, value)
            keep_factor(side, index, rows, value)
    for rows in parts:
        for side in range(2):
            keep(power.at[0, side], rows, product3(factor.at[side], factor.at[side], rows))
    for rows in parts:
        for side in range(2):
            keep(root.at[side], rows, product3(x.at[side], factor.at[side], rows))
    for rows in parts:
        for side in range(2):
            keep(power.at[1, side], rows, product3(power.at[0, side], power.at[0, side], rows))
    for index, rows in enumerate(parts):
        for side in range(2):
            keep_factor(side, index, rows, product3(power.at[1, side], moment.at[side], rows))
    for rows in parts:
        for side in range(2):
            value = product3(factor.at[side], factor.at[side], rows)
            keep(power.at[0, side], rows, value)
            keep(power.at[1, side], rows, value - five_quarters(side, rows))
    for rows in parts:
        for side in range(2):
            keep(moment.at[side], rows, product3(power.at[0, side], power.at[1, side], rows))
    for rows in parts:
        for side in range(2):
            value = product3(power.at[0, side], moment.at[side], rows)
            keep(stat.at[side], rows, value + five_quarters(side, rows))
    last = power.at[1]
    writes = []
    for side in range(2):
        for rows in parts:
            value = product3(root.at[side], stat.at[side], rows)
            final[side, rows, :] = value
            keep(last.at[side], rows, value)
        write = pltpu.make_async_copy(final.at[side], roots.at[side], sems.at[side])
        write.start()
        writes.append(write)
    for rows in cut(width, 2):
        keep(mixed, rows, product3(last.at[0], mean, rows))
    for rows in cut(width, 2):
        out[rows, :] = product3(mixed, last.at[1], rows).astype(BF16)
    for write in writes:
        write.wait()


def refresh(arrived, powers):
    n_micro, width = arrived.shape[0], arrived.shape[-1]
    matrix = (2, 2, width, width)
    return pl.pallas_call(
        refresh_kernel,
        out_shape=(
            jax.ShapeDtypeStruct((2, width, width), F32),
            jax.ShapeDtypeStruct((width, width), BF16),
        ),
        in_specs=[ANY, ANY],
        out_specs=(ANY, VMEM),
        scratch_shapes=[
            pltpu.VMEM((n_micro, width, width), BF16),
            pltpu.VMEM(matrix, BF16),
            pltpu.VMEM(matrix, BF16),
            pltpu.VMEM(matrix, BF16),
            pltpu.VMEM(matrix, BF16),
            pltpu.VMEM(matrix, BF16),
            pltpu.VMEM((2,) + matrix, BF16),
            pltpu.VMEM(matrix, BF16),
            pltpu.VMEM((2, width, width), F32),
            pltpu.VMEM((2, width, width), BF16),
            pltpu.VMEM((2, width, width), BF16),
            pltpu.SemaphoreType.DMA((n_micro + 2,)),
        ],
        compiler_params=pltpu.CompilerParams(vmem_limit_bytes=53 * MB),
        cost_estimate=pl.CostEstimate(
            flops=(20 * 3 + 8) * 2 * width**3, bytes_accessed=9 * MB, transcendentals=0
        ),
        name="refresh_roots",
    )(arrived, powers)


def place_kernel(owners, offsets, order, *refs):
    pieces, (out, sems) = refs[: len(offsets)], refs[-2:]
    n_data, mine = lax.axis_size("dp"), lax.axis_index("dp")
    for number, (piece, (by, skip)) in enumerate(zip(pieces, offsets)):
        base = lax.rem(mine + by, n_data) * owners + skip
        for i in range(piece.shape[0]):
            pltpu.make_async_copy(
                piece.at[i], out.at[order[base + i]], sems.at[number]
            ).start()
    for number, piece in enumerate(pieces):
        pltpu.make_async_copy(piece, out.at[pl.ds(0, piece.shape[0])], sems.at[number]).wait()


def place(owners, order, batch, base):
    offsets, pieces = zip(*batch)
    rows, width = pieces[0].shape[1:]
    count = len(pieces)
    args, specs, aliases = [order, *pieces], [SMEM] + [VMEM] * count, {}
    if base is not None:
        args.append(base)
        specs.append(ANY)
        aliases = {count + 1: 0}
    return pl.pallas_call(
        functools.partial(place_kernel, owners, offsets),
        out_shape=jax.ShapeDtypeStruct((order.shape[0], rows, width), BF16),
        in_specs=specs,
        out_specs=ANY,
        scratch_shapes=[pltpu.SemaphoreType.DMA((count,))],
        input_output_aliases=aliases,
        compiler_params=pltpu.CompilerParams(vmem_limit_bytes=8 * MB),
        cost_estimate=pl.CostEstimate(
            flops=0, bytes_accessed=4 * sum(p.size for p in pieces), transcendentals=0
        ),
        name="place_blocks",
    )(*args)


def body(grads, order, prev_roots):
    n_data = lax.axis_size("dp")
    local = grads[0]
    rows, width = local.shape[1:]
    outgoing = local.at[order].get(
        mode="promise_in_bounds", unique_indices=True, wrap_negative_indices=False
    )
    arrived = lax.all_to_all(outgoing, ("dp", "fsdp"), split_axis=0, concat_axis=0, tiled=True)
    powers = fourth_powers(prev_roots[0])
    roots, refreshed = refresh(arrived.reshape(n_data, width, width), powers)
    pieces = refreshed.reshape(width // rows, rows, width)
    mine = lax.all_to_all(pieces, "fsdp", split_axis=0, concat_axis=0, tiled=True)
    owners = mine.shape[0]
    half = owners // 2

    def shift(value, by):
        return lax.ppermute(value, "dp", [(i, (i + by) % n_data) for i in range(n_data)])

    low, high = mine[:half], mine[half:]
    low_up, high_down = shift(low, 1), shift(high, -1)
    high_up, low_down = shift(high, 1), shift(low, -1)
    low_far, high_far = shift(low_up, 1), shift(high_down, -1)
    result = None
    for batch in (
        (((0, 0), mine), ((n_data - 1, 0), low_up), ((1, half), high_down)),
        (((n_data - 1, half), high_up), ((1, 0), low_down)),
        (((n_data - 2, 0), low_far), ((2, half), high_far)),
    ):
        result = place(owners, order, batch, result)
    return (result, roots[None])


def solution(mesh):
    return jax.shard_map(
        body,
        mesh=mesh,
        in_specs=(P("dp", None, "fsdp", None), P(), P(("dp", "fsdp"), None, None, None)),
        out_specs=(P(None, "fsdp", None), P(("dp", "fsdp"), None, None, None)),
        check_vma=False,
    )
```
